512 devices in a mesh: row: 8 (over z_lo), col: 16 (over z_hi, x, core), dp: 4 (over y).
Axes of the slice: x: 4, y: 4, z: 16 (z_hi: 2, z_lo: 8; z = z_hi * 8 + z_lo), core: 2. Of those that a mesh axis runs over, the one named last changes fastest.
Arguments:
- tokens: bfloat16 [640, 6144], P(('col', 'dp'), 'row'), may hold values from -6 to 6
- in_weight: bfloat16 [6144, 24576], P('row', ('col', 'dp')), may hold values from -0.078125 to 0.078125
- out_weight: bfloat16 [24576, 6144], P(('col', 'dp'), 'row'), may hold values from -0.0390625 to 0.0390625
- cotangent: bfloat16 [640, 6144], P(('col', 'dp'), 'row'), may hold values from -1.5 to 1.5
Outputs:
- mixed: bfloat16 [640, 6144], P(('col', 'dp'), 'row')
- token_grad: bfloat16 [640, 6144], P(('col', 'dp'), 'row')
- in_grad: float32 [6144, 24576], P('row', ('col', 'dp'))
- out_grad: float32 [24576, 6144], P(('col', 'dp'), 'row')
The draws below stay inside these ranges and needn't reach their ends.
All inputs are finite; a program needn't handle non-finite values.
Results may differ from the reference program's by a relative error of at most 0.02.
Values may be sent and summed in bfloat16 or wider, within the bound.
No kernel may reach another device: no remote copies, remote signals or barrier semaphores. Data moves between devices by JAX's collectives and lax.ppermute only.
A program may use at most 64 MiB of HBM per device.

```python
import jax
import jax.numpy as jnp
from jax import lax

D = 6144
FF = 24576
TOKENS = 640
N_ROW = 8


def block_levels(stream_key, shape, pieces, smallest, high):
    gain, own = 1.0, jax.random.fold_in(stream_key, 6)
    for axis_at, shards_of in pieces:
        steps = jnp.exp(jax.random.uniform(jax.random.fold_in(own, axis_at), (shards_of,), jnp.float32, smallest / len(pieces), high / len(pieces)))
        gain = gain * jnp.repeat(steps, shape[axis_at] // shards_of).reshape([-1 if axis == axis_at else 1 for axis in range(len(shape))])
    return gain


def bell_draw(stream_key, extent, spread, most, shards=(), dtype=jnp.bfloat16):
    level = block_levels(stream_key, extent, shards, -0.22, 0.18) if shards else 1.0
    values = jax.random.normal(stream_key, extent, jnp.float32) * spread * level
    return jnp.minimum(jnp.maximum(values, -most), most).astype(dtype)


def setup_inputs(seed: int = 0) -> dict:
    key_of = jax.random.split(jax.random.key(seed), 5)
    tokens = bell_draw(key_of[0], (TOKENS, D), 1.0, 6.0, ((0, 64), (1, 8)))
    in_weight = bell_draw(key_of[1], (D, FF), D ** -0.5, 0.078125, ((0, 8), (1, 64)))
    out_weight = bell_draw(key_of[2], (FF, D), FF ** -0.5, 0.0390625, ((0, 64), (1, 8)))
    cotangent = bell_draw(key_of[3], (TOKENS, D), 0.25, 1.5, ((0, 64), (1, 8)))
    return {"tokens": tokens, "in_weight": in_weight, "out_weight": out_weight, "cotangent": cotangent}


def gelu_value(h):
    inner = 0.7978845608 * (h + 0.044715 * h * h * h)
    return 0.5 * h * (1.0 + jnp.tanh(inner))


def gelu_slope(h):
    inner = 0.7978845608 * (h + 0.044715 * h * h * h)
    t = jnp.tanh(inner)
    return 0.5 * (1.0 + t) + 0.5 * h * (1.0 - t * t) * 0.7978845608 * (1.0 + 3.0 * 0.044715 * h * h)


def blocked_sum(left, right, right_dim):
    width = left.shape[1] // N_ROW
    total = None
    for index in range(N_ROW):
        piece = left[:, index * width:(index + 1) * width]
        if right_dim == 0:
            other = right[index * width:(index + 1) * width, :]
            term = jnp.dot(piece, other, preferred_element_type=jnp.float32)
        else:
            other = right[:, index * width:(index + 1) * width]
            term = lax.dot_general(piece, other, (((1,), (1,)), ((), ())), preferred_element_type=jnp.float32)
        rounded = lax.optimization_barrier(term.astype(jnp.bfloat16))
        term_back = rounded.astype(jnp.float32)
        total = term_back if total is None else total + term_back
    return total


def reference(tokens, in_weight, out_weight, cotangent):
    hidden = blocked_sum(tokens, in_weight, 0)
    acts = gelu_value(hidden).astype(jnp.bfloat16)
    mixed = (tokens.astype(jnp.float32) + jnp.dot(acts, out_weight, preferred_element_type=jnp.float32)).astype(jnp.bfloat16)
    act_grad = blocked_sum(cotangent, out_weight, 1)
    hid_grad = (act_grad * gelu_slope(hidden)).astype(jnp.bfloat16)
    back = lax.dot_general(hid_grad, in_weight, (((1,), (1,)), ((), ())), preferred_element_type=jnp.float32)
    token_grad = (cotangent.astype(jnp.float32) + back).astype(jnp.bfloat16)
    in_grad = lax.dot_general(tokens, hid_grad, (((0,), (0,)), ((), ())), preferred_element_type=jnp.float32)
    out_grad = lax.dot_general(acts, cotangent, (((0,), (0,)), ((), ())), preferred_element_type=jnp.float32)
    return mixed, token_grad, in_grad, out_grad
```

```python
import jax
import jax.numpy as jnp
from jax import lax
from jax.experimental import pallas as pl
from jax.experimental.pallas import tpu as pltpu
from jax.sharding import Mesh
from jax.sharding import PartitionSpec as P

ROW = ("za", "zb", "zc")
CD = ("zhi", "x", "core", "y")
XY = ("x", "y")
SWAP = [(0, 1), (1, 0)]
F32 = jnp.float32
BF16 = jnp.bfloat16
NT = (((1,), (1,)), ((), ()))
TN = (((0,), (0,)), ((), ()))


def gelu_value(h):
    inner = 0.7978845608 * (h + 0.044715 * h * h * h)
    return 0.5 * h * (1.0 + jnp.tanh(inner))


def gelu_slope(h):
    inner = 0.7978845608 * (h + 0.044715 * h * h * h)
    t = jnp.tanh(inner)
    return 0.5 * (1.0 + t) + 0.5 * h * (1.0 - t * t) * 0.7978845608 * (1.0 + 3.0 * 0.044715 * h * h)


def first_kernel(place, x, a, b, send, keep, ordered):
    r, role = place[0], place[1]
    rows = x.shape[1]
    half = 4 * rows
    width = a.shape[2]
    for j in range(8):
        ordered[rows * j : rows * (j + 1), :] = x[lax.bitwise_xor(r, j)]

    @pl.when(role == 0)
    def _():
        for c in range(2):
            cols = slice(width * c, width * (c + 1))
            send[:, cols] = jnp.dot(ordered[half:, :], a[c], preferred_element_type=F32).astype(BF16)
            keep[:, cols] = jnp.dot(ordered[:half, :], a[c], preferred_element_type=F32)

    @pl.when(role == 1)
    def _():
        for c in range(2):
            cols = slice(width * c, width * (c + 1))
            part = b[cols, :]
            send[:, cols] = lax.dot_general(ordered[half:, :], part, NT, preferred_element_type=F32).astype(BF16)
            keep[:, cols] = lax.dot_general(ordered[:half, :], part, NT, preferred_element_type=F32)


def second_kernel(place, low, high, a, b, out):
    r, role = place[0], place[1]
    rows = out.shape[1]
    width = a.shape[2]

    def put(first, product):
        for j in range(4):
            out[lax.bitwise_xor(r, first + j)] = product[rows * j : rows * (j + 1), :].astype(BF16)

    for first, g in ((0, low), (4, high)):

        @pl.when(role == 0)
        def _():
            put(first, jnp.dot(g[...], b[...], preferred_element_type=F32))

        @pl.when(role == 1)
        def _():
            put(
                first,
                lax.dot_general(g[:, :width], a[0], NT, preferred_element_type=F32)
                + lax.dot_general(g[:, width:], a[1], NT, preferred_element_type=F32),
            )


def call(kernel, outs, place, *arrays):
    whole = pl.BlockSpec(memory_space=pltpu.VMEM)
    return pl.pallas_call(
        kernel,
        out_shape=outs,
        in_specs=[pl.BlockSpec(memory_space=pltpu.SMEM)] + [whole] * len(arrays),
        out_specs=jax.tree.map(lambda _: whole, outs),
        compiler_params=pltpu.CompilerParams(vmem_limit_bytes=40 * 1024 * 1024),
        cost_estimate=pl.CostEstimate(flops=2 * 640 * 768 * 768, bytes_accessed=6_000_000, transcendentals=0),
    )(place, *arrays)


def swap(x, axis):
    return lax.ppermute(x, axis, SWAP)


def body(tokens, in_weight, out_weight, cotangent):
    kept, feats = tokens.shape
    width = in_weight.shape[1]
    core = lax.axis_index("core")
    r = 4 * lax.axis_index("zc") + 2 * lax.axis_index("zb") + lax.axis_index("za")
    place = jnp.stack([r, core]).astype(jnp.int32)
    is_first = core == 0

    both = lax.all_gather(jnp.concatenate([tokens, cotangent], axis=1), "core", tiled=True)
    mine = jnp.where(is_first, both[:, :feats], both[:, feats:])
    pair = jnp.concatenate([mine, swap(mine, "zhi")], axis=0)
    a = lax.all_gather(in_weight, "core")
    b = lax.all_gather(out_weight, "core", tiled=True)
    panel = lax.all_to_all(jnp.broadcast_to(pair[None], (16,) + pair.shape), XY, 0, 0, tiled=True)
    panel = panel.reshape(8, 8 * kept, feats)
    rows = 8 * kept

    send, keep, ordered = call(
        first_kernel,
        (
            jax.ShapeDtypeStruct((4 * rows, 2 * width), BF16),
            jax.ShapeDtypeStruct((4 * rows, 2 * width), F32),
            jax.ShapeDtypeStruct((8 * rows, feats), BF16),
        ),
        place,
        panel,
        a,
        b,
    )
    panels = lax.all_gather(ordered, "core")

    for axis, count in (("zc", 2), ("zb", 1), ("za", 0)):
        came = swap(send, axis)
        if count:
            cut = count * rows
            send = (keep[cut:] + came[cut:].astype(F32)).astype(BF16)
            keep = keep[:cut] + came[:cut].astype(F32)
        else:
            keep = keep + came.astype(F32)

    other = swap(keep, "core")
    block = jnp.where(is_first, gelu_value(keep), keep * gelu_slope(other)).astype(BF16)

    block = jnp.concatenate([block, swap(block, "za")], axis=0)
    block = jnp.concatenate([block, swap(block, "zb")], axis=0)
    high = swap(block, "zc")

    part = call(second_kernel, jax.ShapeDtypeStruct((8, rows, feats), BF16), place, block, high, a, b)
    grads = lax.all_gather(jnp.concatenate([block, high], axis=0), "core")

    parts = lax.all_to_all(part.reshape(16, 4 * kept, feats), XY, 0, 0, tiled=True)
    sums = jnp.sum(parts.astype(F32), axis=0)
    sums = sums[: 2 * kept] + swap(sums[2 * kept :].astype(BF16), "zhi").astype(F32)
    got = swap(jnp.where(is_first, sums[kept:], sums[:kept]), "core")
    mixed = (tokens.astype(F32) + jnp.where(is_first, sums[:kept], got)).astype(BF16)
    token_grad = (cotangent.astype(F32) + jnp.where(is_first, got, sums[kept:])).astype(BF16)

    acts = lax.dynamic_slice_in_dim(grads[0], core * width, width, axis=1)
    hid_grad = lax.dynamic_slice_in_dim(grads[1], core * width, width, axis=1)
    in_grad = lax.dot_general(panels[0], hid_grad, TN, preferred_element_type=F32)
    out_grad = lax.dot_general(acts, panels[1], TN, preferred_element_type=F32)
    return (mixed, token_grad, in_grad, out_grad)


def solution(mesh):
    fine = Mesh(mesh.devices.reshape(2, 2, 2, 2, 4, 2, 4), ROW + CD)
    return jax.shard_map(
        body,
        mesh=fine,
        in_specs=(P(CD, ROW), P(ROW, CD), P(CD, ROW), P(CD, ROW)),
        out_specs=(P(CD, ROW), P(CD, ROW), P(ROW, CD), P(CD, ROW)),
        check_vma=False,
    )
```

```python
import jax
import jax.numpy as jnp
from jax import lax
from jax.experimental import pallas as pl
from jax.experimental.pallas import tpu as pltpu
from jax.sharding import Mesh
from jax.sharding import PartitionSpec as P

ROW = ("za", "zb", "zc")
QUAD = ("zb", "zc")
CD = ("zhi", "x", "core", "y")
XY = ("x", "y")
CHIPS = ("zhi", "core")
SWAP = [(0, 1), (1, 0)]
F32 = jnp.float32
BF16 = jnp.bfloat16
NT = (((1,), (1,)), ((), ()))
TN = (((0,), (0,)), ((), ()))


def gelu_value(h):
    inner = 0.7978845608 * (h + 0.044715 * h * h * h)
    return 0.5 * h * (1.0 + jnp.tanh(inner))


def gelu_slope(h):
    inner = 0.7978845608 * (h + 0.044715 * h * h * h)
    t = jnp.tanh(inner)
    return 0.5 * (1.0 + t) + 0.5 * h * (1.0 - t * t) * 0.7978845608 * (1.0 + 3.0 * 0.044715 * h * h)


def dot(left, right, dims=(((1,), (0,)), ((), ()))):
    return lax.dot_general(left, right, dims, preferred_element_type=F32)


def first_kernel(core, x, own_in, got_in, own_out, got_out, out):
    width = own_in.shape[1]

    @pl.when(core[0] == 0)
    def _():
        out[:, :width] = dot(x[...], own_in[...]).astype(BF16)
        out[:, width:] = dot(x[...], got_in[...]).astype(BF16)

    @pl.when(core[0] == 1)
    def _():
        out[:, :width] = dot(x[...], got_out[...], NT).astype(BF16)
        out[:, width:] = dot(x[...], own_out[...], NT).astype(BF16)


def second_kernel(core, g, own_in, got_in, own_out, got_out, out, give):
    width = own_in.shape[1]

    @pl.when(core[0] == 0)
    def _():
        out[...] = (dot(g[:, :width], own_out[...]) + dot(g[:, width:], got_out[...])).astype(BF16)
        give[...] = g[:, width:]

    @pl.when(core[0] == 1)
    def _():
        out[...] = (dot(g[:, :width], got_in[...], NT) + dot(g[:, width:], own_in[...], NT)).astype(BF16)
        give[...] = g[:, :width]


def grads_kernel(core, x, y, g, k, in_grad, out_grad):
    width = k.shape[1]

    @pl.when(core[0] == 0)
    def _():
        in_grad[...] = dot(x[...], k[...], TN)
        out_grad[...] = dot(g[:, :width], y[...], TN)

    @pl.when(core[0] == 1)
    def _():
        in_grad[...] = dot(y[...], g[:, width:], TN)
        out_grad[...] = dot(k[...], x[...], TN)


def call(kernel, outs, core, *arrays):
    whole = pl.BlockSpec(memory_space=pltpu.VMEM)
    return pl.pallas_call(
        kernel,
        out_shape=outs,
        in_specs=[pl.BlockSpec(memory_space=pltpu.SMEM)] + [whole] * len(arrays),
        out_specs=jax.tree.map(lambda _: whole, outs),
        compiler_params=pltpu.CompilerParams(vmem_limit_bytes=40 * 1024 * 1024),
        cost_estimate=pl.CostEstimate(flops=2 * 640 * 768 * 768, bytes_accessed=5_000_000, transcendentals=0),
    )(core, *arrays)


def swap(x, axis):
    return lax.ppermute(x, axis, SWAP)


def body(tokens, in_weight, out_weight, cotangent):
    kept, feats = tokens.shape
    width = in_weight.shape[1]
    core, zhi = lax.axis_index("core"), lax.axis_index("zhi")
    is_first = core == 0
    low = lax.axis_index("za") == 0
    place = core.astype(jnp.int32).reshape(1)
    spread, four = 16, 4 * kept
    count = spread * four
    eighth = count // 8
    struct = jax.ShapeDtypeStruct

    both = lax.all_gather(jnp.concatenate([tokens, cotangent], axis=1), CHIPS, tiled=True)
    group = jnp.where(is_first, both[:, :feats], both[:, feats:])
    block = jnp.broadcast_to(group[None], (spread,) + group.shape)
    x = lax.all_to_all(block, XY, 0, 0, tiled=True).reshape(count, feats)
    weights = (in_weight, swap(in_weight, "core"), out_weight, swap(out_weight, "core"))

    part = call(first_kernel, struct((count, 2 * width), BF16), place, x, *weights)
    parts = lax.all_to_all(part.reshape(4, count // 4, 2 * width), QUAD, 0, 0, tiled=True)
    near = jnp.sum(parts.astype(F32), axis=0)
    sent = lax.all_gather(jnp.where(low, near[eighth:], near[:eighth]).astype(BF16), "za")
    full = jnp.where(low, near[:eighth], near[eighth:]) + jnp.where(low, sent[1], sent[0]).astype(F32)
    hidden = lax.all_gather(full.astype(BF16), "core")[0].astype(F32)
    shard = jnp.where(is_first, gelu_value(full), full * gelu_slope(hidden)).astype(BF16)
    shard = lax.all_gather(shard, "za", tiled=True)
    g = lax.all_gather(shard, QUAD, tiled=True)

    shapes = (struct((count, feats), BF16), struct((count, width), BF16))
    out, give = call(second_kernel, shapes, place, g, *weights)
    parts = lax.all_to_all(out.reshape(spread, four, feats), XY, 0, 0, tiled=True)
    y = swap(x, "core")
    k = swap(give, "core")
    shapes = (struct((feats, width), F32), struct((width, feats), F32))
    in_grad, out_grad = call(grads_kernel, shapes, place, x, y, g, k)
    sums = jnp.sum(parts.astype(F32), axis=0).astype(BF16)
    sums, in_grad, out_grad = lax.optimization_barrier((sums, in_grad, out_grad))
    sums = lax.all_gather(sums, CHIPS).reshape(2, 2, 4, kept, feats)
    sums = lax.dynamic_index_in_dim(sums, 2 * zhi + core, axis=2, keepdims=False).astype(F32)
    sums = sums[0] + sums[1]
    mixed = (tokens.astype(F32) + sums[0]).astype(BF16)
    token_grad = (cotangent.astype(F32) + sums[1]).astype(BF16)
    return (mixed, token_grad, in_grad, out_grad)


def solution(mesh):
    fine = Mesh(mesh.devices.reshape(2, 2, 2, 2, 4, 2, 4), ROW + CD)
    return jax.shard_map(
        body,
        mesh=fine,
        in_specs=(P(CD, ROW), P(ROW, CD), P(CD, ROW), P(CD, ROW)),
        out_specs=(P(CD, ROW), P(CD, ROW), P(ROW, CD), P(CD, ROW)),
        check_vma=False,
    )
```

```python
import jax
import jax.numpy as jnp
from jax import lax
from jax.experimental import pallas as pl
from jax.experimental.pallas import tpu as pltpu
from jax.sharding import Mesh
from jax.sharding import PartitionSpec as P

ROW = ("za", "zb", "zc")
QUAD = ("zb", "zc")
CD = ("zhi", "x", "core", "y")
XY = ("x", "y")
CHIPS = ("zhi", "core")
SWAP = [(0, 1), (1, 0)]
F32 = jnp.float32
BF16 = jnp.bfloat16
NT = (((1,), (1,)), ((), ()))
TN = (((0,), (0,)), ((), ()))


def gelu_value(h):
    inner = 0.7978845608 * (h + 0.044715 * h * h * h)
    return 0.5 * h * (1.0 + jnp.tanh(inner))


def gelu_slope(h):
    inner = 0.7978845608 * (h + 0.044715 * h * h * h)
    t = jnp.tanh(inner)
    return 0.5 * (1.0 + t) + 0.5 * h * (1.0 - t * t) * 0.7978845608 * (1.0 + 3.0 * 0.044715 * h * h)


def dot(left, right, dims=(((1,), (0,)), ((), ()))):
    return lax.dot_general(left, right, dims, preferred_element_type=F32)


def first_kernel(place, x, own_in, got_in, own_out, got_out, out, rows):
    width = own_in.shape[1]
    size = x.shape[2]
    for q in range(x.shape[0]):
        rows[size * q : size * (q + 1), :] = x[q, place[1]]

    @pl.when(place[0] == 0)
    def _():
        out[:, :width] = dot(rows[...], own_in[...]).astype(BF16)
        out[:, width:] = dot(rows[...], got_in[...]).astype(BF16)

    @pl.when(place[0] == 1)
    def _():
        out[:, :width] = dot(rows[...], got_out[...], NT).astype(BF16)
        out[:, width:] = dot(rows[...], own_out[...], NT).astype(BF16)


def second_kernel(core, g, own_in, got_in, own_out, got_out, out, give):
    width = own_in.shape[1]

    @pl.when(core[0] == 0)
    def _():
        out[...] = (dot(g[:, :width], own_out[...]) + dot(g[:, width:], got_out[...])).astype(BF16)
        give[...] = g[:, width:]

    @pl.when(core[0] == 1)
    def _():
        out[...] = (dot(g[:, :width], got_in[...], NT) + dot(g[:, width:], own_in[...], NT)).astype(BF16)
        give[...] = g[:, :width]


def grads_kernel(core, x, y, g, k, in_grad, out_grad):
    width = k.shape[1]

    @pl.when(core[0] == 0)
    def _():
        in_grad[...] = dot(x[...], k[...], TN)
        out_grad[...] = dot(g[:, :width], y[...], TN)

    @pl.when(core[0] == 1)
    def _():
        in_grad[...] = dot(y[...], g[:, width:], TN)
        out_grad[...] = dot(k[...], x[...], TN)


def call(kernel, outs, core, *arrays, scratch=()):
    whole = pl.BlockSpec(memory_space=pltpu.VMEM)
    return pl.pallas_call(
        kernel,
        out_shape=outs,
        in_specs=[pl.BlockSpec(memory_space=pltpu.SMEM)] + [whole] * len(arrays),
        out_specs=jax.tree.map(lambda _: whole, outs),
        scratch_shapes=scratch,
        compiler_params=pltpu.CompilerParams(vmem_limit_bytes=40 * 1024 * 1024),
        cost_estimate=pl.CostEstimate(flops=2 * 640 * 768 * 768, bytes_accessed=5_000_000, transcendentals=0),
    )(core, *arrays)


def swap(x, axis):
    return lax.ppermute(x, axis, SWAP)


def tie(*arrays):
    return lax.optimization_barrier(arrays)


def body(tokens, in_weight, out_weight, cotangent):
    kept, feats = tokens.shape
    width = in_weight.shape[1]
    core, zhi, za = lax.axis_index("core"), lax.axis_index("zhi"), lax.axis_index("za")
    is_first = core == 0
    place = core.astype(jnp.int32).reshape(1)
    spread, four = 16, 4 * kept
    count = spread * four
    half, eighth = count // 2, count // 8
    struct = jax.ShapeDtypeStruct

    both = lax.all_gather(jnp.concatenate([tokens, cotangent], axis=1), CHIPS, tiled=True)
    group = jnp.where(is_first, both[:, :feats], both[:, feats:])
    block = jnp.broadcast_to(group[None], (spread,) + group.shape)
    x = lax.all_to_all(block, XY, 0, 0, tiled=True).reshape(count, feats)
    weights = (in_weight, swap(in_weight, "core"), out_weight, swap(out_weight, "core"))

    def terms(which):
        out = call(
            first_kernel,
            struct((half, 2 * width), BF16),
            jnp.stack([core, which]).astype(jnp.int32),
            x.reshape(4, 2, eighth, feats),
            *weights,
            scratch=[pltpu.VMEM((half, feats), BF16)],
        )
        return out.reshape(4, eighth, 2 * width)

    def exchange(blocks):
        return lax.all_to_all(blocks, QUAD, 0, 0, tiled=True)

    def total(parts):
        return jnp.sum(parts.astype(F32), axis=0)

    far, near, y = tie(exchange(terms(1 - za)), terms(za), swap(x, "core"))
    came = swap(total(far).astype(BF16), "za")
    full = total(exchange(near)) + came.astype(F32)
    hidden = lax.all_gather(full.astype(BF16), "core")[0].astype(F32)
    shard = jnp.where(is_first, gelu_value(full), full * gelu_slope(hidden)).astype(BF16)
    shard = lax.all_gather(shard, "za", tiled=True)
    g = lax.all_gather(shard, QUAD, tiled=True)

    shapes = (struct((count, feats), BF16), struct((count, width), BF16))
    out, give = call(second_kernel, shapes, place, g, *weights)
    parts = lax.all_to_all(out.reshape(spread, four, feats), XY, 0, 0, tiled=True)
    k = swap(give, "core")
    shapes = (struct((feats, width), F32), struct((width, feats), F32))
    in_grad, out_grad = call(grads_kernel, shapes, place, x, y, g, k)
    parts, in_grad, out_grad = tie(parts, in_grad, out_grad)
    sums = lax.all_gather(total(parts).astype(BF16), CHIPS).reshape(2, 2, 4, kept, feats)
    sums = lax.dynamic_index_in_dim(sums, 2 * zhi + core, axis=2, keepdims=False).astype(F32)
    sums = sums[0] + sums[1]
    mixed = (tokens.astype(F32) + sums[0]).astype(BF16)
    token_grad = (cotangent.astype(F32) + sums[1]).astype(BF16)
    return (mixed, token_grad, in_grad, out_grad)


def solution(mesh):
    fine = Mesh(mesh.devices.reshape(2, 2, 2, 2, 4, 2, 4), ROW + CD)
    return jax.shard_map(
        body,
        mesh=fine,
        in_specs=(P(CD, ROW), P(ROW, CD), P(CD, ROW), P(CD, ROW)),
        out_specs=(P(CD, ROW), P(CD, ROW), P(ROW, CD), P(CD, ROW)),
        check_vma=False,
    )
```

```python
import functools

import jax
import jax.numpy as jnp
from jax import lax
from jax.experimental import pallas as pl
from jax.experimental.pallas import tpu as pltpu
from jax.sharding import Mesh
from jax.sharding import PartitionSpec as P

ROW = ("za", "zb", "zc")
QUAD = ("zb", "zc")
CD = ("zhi", "x", "core", "y")
XY = ("x", "y")
CHIPS = ("zhi", "core")
SWAP = [(0, 1), (1, 0)]
CUTS = (0, 6, 10)
F32 = jnp.float32
BF16 = jnp.bfloat16
NT = (((1,), (1,)), ((), ()))
TN = (((0,), (0,)), ((), ()))


def gelu_value(h):
    inner = 0.7978845608 * (h + 0.044715 * h * h * h)
    return 0.5 * h * (1.0 + jnp.tanh(inner))


def gelu_slope(h):
    inner = 0.7978845608 * (h + 0.044715 * h * h * h)
    t = jnp.tanh(inner)
    return 0.5 * (1.0 + t) + 0.5 * h * (1.0 - t * t) * 0.7978845608 * (1.0 + 3.0 * 0.044715 * h * h)


def dot(left, right, dims=(((1,), (0,)), ((), ()))):
    return lax.dot_general(left, right, dims, preferred_element_type=F32)


def first_kernel(low, high, place, x, own_in, got_in, own_out, got_out, out, rows):
    width = own_in.shape[1]
    size = high - low
    for q in range(x.shape[0]):
        rows[size * q : size * (q + 1), :] = x[q, low:high]

    @pl.when(place[0] == 0)
    def _():
        out[:, :width] = dot(rows[...], own_in[...]).astype(BF16)
        out[:, width:] = dot(rows[...], got_in[...]).astype(BF16)

    @pl.when(place[0] == 1)
    def _():
        out[:, :width] = dot(rows[...], got_out[...], NT).astype(BF16)
        out[:, width:] = dot(rows[...], own_out[...], NT).astype(BF16)


def second_kernel(core, g, own_in, got_in, own_out, got_out, out):
    width = own_in.shape[1]

    @pl.when(core[0] == 0)
    def _():
        out[...] = (dot(g[:, :width], own_out[...]) + dot(g[:, width:], got_out[...])).astype(BF16)

    @pl.when(core[0] == 1)
    def _():
        out[...] = (dot(g[:, :width], got_in[...], NT) + dot(g[:, width:], own_in[...], NT)).astype(BF16)


def grads_kernel(core, x, y, g, k, in_grad, out_grad):
    width = k.shape[1]

    @pl.when(core[0] == 0)
    def _():
        in_grad[...] = dot(x[...], k[...], TN)
        out_grad[...] = dot(g[:, :width], y[...], TN)

    @pl.when(core[0] == 1)
    def _():
        in_grad[...] = dot(y[...], g[:, width:], TN)
        out_grad[...] = dot(k[...], x[...], TN)


def call(kernel, outs, core, *arrays, scratch=()):
    whole = pl.BlockSpec(memory_space=pltpu.VMEM)
    return pl.pallas_call(
        kernel,
        out_shape=outs,
        in_specs=[pl.BlockSpec(memory_space=pltpu.SMEM)] + [whole] * len(arrays),
        out_specs=jax.tree.map(lambda _: whole, outs),
        scratch_shapes=scratch,
        compiler_params=pltpu.CompilerParams(vmem_limit_bytes=40 * 1024 * 1024),
        cost_estimate=pl.CostEstimate(flops=2 * 640 * 768 * 768, bytes_accessed=5_000_000, transcendentals=0),
    )(core, *arrays)


def swap(x, axis):
    return lax.ppermute(x, axis, SWAP)


def tie(*arrays):
    return lax.optimization_barrier(arrays)


def body(tokens, in_weight, out_weight, cotangent):
    kept, feats = tokens.shape
    width = in_weight.shape[1]
    core, zhi = lax.axis_index("core"), lax.axis_index("zhi")
    is_first = core == 0
    place = core.astype(jnp.int32).reshape(1)
    spread, four = 16, 4 * kept
    count = spread * four
    quarter = count // 4
    struct = jax.ShapeDtypeStruct

    both = lax.all_gather(jnp.concatenate([tokens, cotangent], axis=1), CHIPS, tiled=True)
    group = jnp.where(is_first, both[:, :feats], both[:, feats:])
    block = jnp.broadcast_to(group[None], (spread,) + group.shape)
    x = lax.all_to_all(block, XY, 0, 0, tiled=True).reshape(count, feats)
    weights = (in_weight, swap(in_weight, "core"), out_weight, swap(out_weight, "core"))

    def terms(low, high):
        size = 4 * (high - low)
        out = call(
            functools.partial(first_kernel, low, high),
            struct((size, 2 * width), BF16),
            place,
            x.reshape(4, quarter, feats),
            *weights,
            scratch=[pltpu.VMEM((size, feats), BF16)],
        )
        return out.reshape(4, high - low, 2 * width)

    def exchange(blocks):
        return lax.all_to_all(blocks, QUAD, 0, 0, tiled=True)

    def total(parts):
        return jnp.sum(parts.astype(F32), axis=0)

    def finish(near, came):
        full = near + came.astype(F32)
        hidden = lax.all_gather(full.astype(BF16), "core")[0].astype(F32)
        return jnp.where(is_first, gelu_value(full), full * gelu_slope(hidden)).astype(BF16)

    cuts = [quarter * tenths // 10 for tenths in CUTS]
    nears, cames, sent = [], [], None
    for low, high in zip(cuts[:-1], cuts[1:]):
        part = terms(low, high)
        if sent is not None:
            sent, part = tie(sent, part)
            nears.append(total(sent))
            cames.append(swap(nears[-1].astype(BF16), "za"))
        sent = exchange(part)
        if low == 0:
            sent, y = tie(sent, swap(x, "core"))
    nears.append(total(sent))
    cames.append(swap(nears[-1].astype(BF16), "za"))
    shard = finish(jnp.concatenate(nears, axis=0), jnp.concatenate(cames, axis=0))
    g = lax.all_gather(shard, QUAD, tiled=True)

    out = call(second_kernel, struct((count, feats), BF16), place, g, *weights)
    parts = lax.all_to_all(out.reshape(spread, four, feats), XY, 0, 0, tiled=True)
    k = swap(jnp.where(is_first, g[:, width:], g[:, :width]), "core")
    shapes = (struct((feats, width), F32), struct((width, feats), F32))
    in_grad, out_grad = call(grads_kernel, shapes, place, x, y, g, k)
    parts, in_grad, out_grad = tie(parts, in_grad, out_grad)
    sums = lax.all_gather(total(parts).astype(BF16), CHIPS).reshape(2, 2, 4, kept, feats)
    sums = lax.dynamic_index_in_dim(sums, 2 * zhi + core, axis=2, keepdims=False).astype(F32)
    sums = sums[0] + sums[1]
    mixed = (tokens.astype(F32) + sums[0]).astype(BF16)
    token_grad = (cotangent.astype(F32) + sums[1]).astype(BF16)
    return (mixed, token_grad, in_grad, out_grad)


def solution(mesh):
    fine = Mesh(mesh.devices.reshape(2, 2, 2, 2, 4, 2, 4), ROW + CD)
    return jax.shard_map(
        body,
        mesh=fine,
        in_specs=(P(CD, ROW), P(ROW, CD), P(CD, ROW), P(CD, ROW)),
        out_specs=(P(CD, ROW), P(CD, ROW), P(ROW, CD), P(CD, ROW)),
        check_vma=False,
    )
```

```python
import functools

import jax
import jax.numpy as jnp
from jax import lax
from jax.experimental import pallas as pl
from jax.experimental.pallas import tpu as pltpu
from jax.sharding import Mesh
from jax.sharding import PartitionSpec as P

ROW = ("za", "zb", "zc")
QUAD = ("zb", "zc")
CD = ("zhi", "x", "core", "y")
XY = ("x", "y")
CHIPS = ("zhi", "core")
SWAP = [(0, 1), (1, 0)]
CUTS = (0, 7, 10)
F32 = jnp.float32
BF16 = jnp.bfloat16
NT = (((1,), (1,)), ((), ()))
TN = (((0,), (0,)), ((), ()))


def gelu_value(h):
    inner = 0.7978845608 * (h + 0.044715 * h * h * h)
    return 0.5 * h * (1.0 + jnp.tanh(inner))


def gelu_slope(h):
    inner = 0.7978845608 * (h + 0.044715 * h * h * h)
    t = jnp.tanh(inner)
    return 0.5 * (1.0 + t) + 0.5 * h * (1.0 - t * t) * 0.7978845608 * (1.0 + 3.0 * 0.044715 * h * h)


def dot(left, right, dims=(((1,), (0,)), ((), ()))):
    return lax.dot_general(left, right, dims, preferred_element_type=F32)


def first_kernel(low, high, place, x, own_in, got_in, own_out, got_out, out, rows):
    width = own_in.shape[1]
    size = high - low
    for q in range(x.shape[0]):
        rows[size * q : size * (q + 1), :] = x[q, low:high]

    @pl.when(place[0] == 0)
    def _():
        out[:, :width] = dot(rows[...], own_in[...]).astype(BF16)
        out[:, width:] = dot(rows[...], got_in[...]).astype(BF16)

    @pl.when(place[0] == 1)
    def _():
        out[:, :width] = dot(rows[...], got_out[...], NT).astype(BF16)
        out[:, width:] = dot(rows[...], own_out[...], NT).astype(BF16)


def second_kernel(core, g, own_in, got_in, own_out, got_out, out):
    width = own_in.shape[1]

    @pl.when(core[0] == 0)
    def _():
        out[...] = (dot(g[:, :width], own_out[...]) + dot(g[:, width:], got_out[...])).astype(BF16)

    @pl.when(core[0] == 1)
    def _():
        out[...] = (dot(g[:, :width], got_in[...], NT) + dot(g[:, width:], own_in[...], NT)).astype(BF16)


def grads_kernel(core, x, y, g, k, in_grad, out_grad):
    width = k.shape[1]

    @pl.when(core[0] == 0)
    def _():
        in_grad[...] = dot(x[...], k[...], TN)
        out_grad[...] = dot(g[:, :width], y[...], TN)

    @pl.when(core[0] == 1)
    def _():
        in_grad[...] = dot(y[...], g[:, width:], TN)
        out_grad[...] = dot(k[...], x[...], TN)


def call(kernel, outs, core, *arrays, scratch=()):
    whole = pl.BlockSpec(memory_space=pltpu.VMEM)
    return pl.pallas_call(
        kernel,
        out_shape=outs,
        in_specs=[pl.BlockSpec(memory_space=pltpu.SMEM)] + [whole] * len(arrays),
        out_specs=jax.tree.map(lambda _: whole, outs),
        scratch_shapes=scratch,
        compiler_params=pltpu.CompilerParams(vmem_limit_bytes=40 * 1024 * 1024),
        cost_estimate=pl.CostEstimate(flops=2 * 640 * 768 * 768, bytes_accessed=5_000_000, transcendentals=0),
    )(core, *arrays)


def swap(x, axis):
    return lax.ppermute(x, axis, SWAP)


def tie(*arrays):
    return lax.optimization_barrier(arrays)


def body(tokens, in_weight, out_weight, cotangent):
    kept, feats = tokens.shape
    width = in_weight.shape[1]
    core, zhi = lax.axis_index("core"), lax.axis_index("zhi")
    is_first = core == 0
    place = core.astype(jnp.int32).reshape(1)
    spread, four = 16, 4 * kept
    count = spread * four
    quarter = count // 4
    struct = jax.ShapeDtypeStruct

    both = lax.all_gather(jnp.concatenate([tokens, cotangent], axis=1), CHIPS, tiled=True)
    group = jnp.where(is_first, both[:, :feats], both[:, feats:])
    block = jnp.broadcast_to(group[None], (spread,) + group.shape)
    x = lax.all_to_all(block, XY, 0, 0, tiled=True).reshape(count, feats)
    weights = (in_weight, swap(in_weight, "core"), out_weight, swap(out_weight, "core"))

    def terms(low, high):
        size = 4 * (high - low)
        out = call(
            functools.partial(first_kernel, low, high),
            struct((size, 2 * width), BF16),
            place,
            x.reshape(4, quarter, feats),
            *weights,
            scratch=[pltpu.VMEM((size, feats), BF16)],
        )
        return out.reshape(4, high - low, 2 * width)

    def exchange(blocks):
        return lax.all_to_all(blocks, QUAD, 0, 0, tiled=True)

    def total(parts):
        return jnp.sum(parts.astype(F32), axis=0)

    def finish(near, came):
        full = near + came.astype(F32)
        hidden = lax.all_gather(full.astype(BF16), "core")[0].astype(F32)
        return jnp.where(is_first, gelu_value(full), full * gelu_slope(hidden)).astype(BF16)

    cuts = [quarter * tenths // 10 for tenths in CUTS]
    nears, cames, sent = [], [], None
    for low, high in zip(cuts[:-1], cuts[1:]):
        part = terms(low, high)
        if sent is not None:
            sent, part = tie(sent, part)
            nears.append(total(sent))
            cames.append(swap(nears[-1].astype(BF16), "za"))
        sent = exchange(part)
        if low == 0:
            sent, y = tie(sent, swap(x, "core"))
    nears.append(total(sent))
    both = lax.all_gather(nears[-1].astype(BF16), "za")
    cames.append(jnp.where(lax.axis_index("za") == 0, both[1], both[0]))
    shard = finish(jnp.concatenate(nears, axis=0), jnp.concatenate(cames, axis=0))
    g = lax.all_gather(shard, QUAD, tiled=True)

    out = call(second_kernel, struct((count, feats), BF16), place, g, *weights)
    parts = lax.all_to_all(out.reshape(spread, four, feats), XY, 0, 0, tiled=True)
    k = swap(jnp.where(is_first, g[:, width:], g[:, :width]), "core")
    shapes = (struct((feats, width), F32), struct((width, feats), F32))
    in_grad, out_grad = call(grads_kernel, shapes, place, x, y, g, k)
    parts, in_grad, out_grad = tie(parts, in_grad, out_grad)
    sums = lax.all_gather(total(parts).astype(BF16), CHIPS).reshape(2, 2, 4, kept, feats)
    sums = lax.dynamic_index_in_dim(sums, 2 * zhi + core, axis=2, keepdims=False).astype(F32)
    sums = sums[0] + sums[1]
    mixed = (tokens.astype(F32) + sums[0]).astype(BF16)
    token_grad = (cotangent.astype(F32) + sums[1]).astype(BF16)
    return (mixed, token_grad, in_grad, out_grad)


def solution(mesh):
    fine = Mesh(mesh.devices.reshape(2, 2, 2, 2, 4, 2, 4), ROW + CD)
    return jax.shard_map(
        body,
        mesh=fine,
        in_specs=(P(CD, ROW), P(ROW, CD), P(CD, ROW), P(CD, ROW)),
        out_specs=(P(CD, ROW), P(CD, ROW), P(ROW, CD), P(CD, ROW)),
        check_vma=False,
    )
```
